32 devices in a mesh: section: 2 (over x), dp: 4 (over z), tensor: 4 (over y, core).
Axes of the slice: x: 2, y: 2, z: 4, core: 2. Of those that a mesh axis runs over, the one named last changes fastest.
Arguments:
- inputs: bfloat16 [2, 16, 208, 768], P(None, ('dp', 'tensor')), may hold values from -6 to 6
- cotangent: bfloat16 [2, 16, 208, 768], P(None, ('dp', 'tensor')), may hold values from -6 to 6
- image_ids: int32 [2, 16, 208], P(None, 'dp'), may hold values from 0 to 3, never falling along the last dimension, each value on 1 to 78 neighbouring positions
- keep_mask: int32 [2, 16, 208], P(None, 'dp'), may hold values from 0 to 1, as said below
- w_qkv: bfloat16 [2, 3, 768, 768], P('section', None, None, 'tensor'), may hold values from -0.21875 to 0.21875
- w_out: bfloat16 [2, 768, 768], P('section', 'tensor'), may hold values from -0.875 to 0.875
- w_up: bfloat16 [2, 768, 3072], P('section', None, 'tensor'), may hold values from -0.21875 to 0.21875
- w_down: bfloat16 [2, 3072, 768], P('section', 'tensor'), may hold values from -0.109375 to 0.109375
- norm_gain: float32 [2, 2, 768], P('section'), may hold values from 0.5 to 1.5
- norm_shift: float32 [2, 2, 768], P('section'), may hold values from -1 to 1
Outputs:
- layer_out: bfloat16 [2, 2, 16, 208, 768], P('section', None, ('dp', 'tensor'))
- input_grad: float32 [2, 2, 16, 208, 768], P('section', None, ('dp', 'tensor'))
- grad_w_qkv: float32 [2, 3, 768, 768], P('section', None, None, 'tensor')
- grad_w_out: float32 [2, 768, 768], P('section', 'tensor')
- grad_w_up: float32 [2, 768, 3072], P('section', None, 'tensor')
- grad_w_down: float32 [2, 3072, 768], P('section', 'tensor')
- grad_gain: float32 [2, 2, 768], P('section')
- grad_shift: float32 [2, 2, 768], P('section')
- counts: int32 [208], replicated
The draws below stay inside these ranges and needn't reach their ends.
Inputs may be any that keep to these rules, and one draw needn't show every extreme that they name: `image_ids`: in each row the ids never fall and each of the 4 images holds 1 to 78 patches, one exactly that many. `keep_mask`: each row has exactly 52 ones.
All inputs are finite; a program needn't handle non-finite values.
Results may differ from the reference program's by a relative error of at most 0.023.
Values may be sent and summed in bfloat16 or wider, within the bound.
A program may use at most 192 MiB of HBM per device.

```python
import math
import jax
import jax.numpy as jnp
import numpy as np
from jax import lax

D = 768
HEADS = 12
HEAD = 64
FF = 3072
L = 208
MB = 2
KEEP = 52
ROWS_ALL = 16


def draw_keep_mask(key, part):
    key = jax.random.fold_in(key, 7)
    random_bits = jax.random.randint(key, (MB, ROWS_ALL, L), 0, 1 << 20)
    distinct = random_bits * L + jnp.arange(L, dtype=jnp.int32)
    ranked = jnp.argsort(jnp.argsort(distinct, axis=-1), axis=-1)
    return (ranked < KEEP).astype(jnp.int32)


def block_levels(stream_key, shape, pieces, low, top_value):
    level, own = 1.0, jax.random.fold_in(stream_key, 6)
    for position, shards_of in pieces:
        draws = jnp.exp(jax.random.uniform(jax.random.fold_in(own, position), (shards_of,), jnp.float32, low / len(pieces), top_value / len(pieces)))
        level = level * jnp.repeat(draws, shape[position] // shards_of).reshape([-1 if axis == position else 1 for axis in range(len(shape))])
    return level


def profile(amount, total, bound, skew):
    portions = [(1 << 20) // math.isqrt(grade ** skew) + 1 for grade in range(2, amount + 1)]
    rest, given = total - bound - (amount - 1), [1] * (amount - 1)
    while rest > 0:
        candidates = [i for i in range(amount - 1) if given[i] < bound]
        pool, remaining = sum([portions[i] for i in candidates]), rest
        for i in candidates:
            more = min(bound - given[i], max(1, remaining * portions[i] // pool), rest)
            given[i] = given[i] + more
            rest = rest - more
    return np.array([bound] + given)


def uneven_parts(stream_key, number_of, total, most, slope):
    if number_of == 2:
        one = jax.random.randint(stream_key, (), max(1, total - most), min(most, total - 1) + 1)
        return jnp.stack([one, total - one])
    tallies = jnp.asarray(profile(number_of, total, most, slope), jnp.int32)
    couples = (number_of - 1) // 2
    giver, receiver = tallies[1:1 + 2 * couples:2], tallies[2:2 + 2 * couples:2]
    margin = jnp.minimum(giver - 1, most - receiver)
    shifted = jax.random.randint(jax.random.fold_in(stream_key, 1), (couples,), 0, 1 << 20) % (margin + 1)
    tallies = tallies.at[1:1 + 2 * couples:2].set(giver - shifted).at[2:2 + 2 * couples:2].set(receiver + shifted)
    return tallies[jax.random.permutation(jax.random.fold_in(stream_key, 2), number_of)]


def scatter_about(stream_key, shape, spread, bound, cuts=(), held_as=jnp.bfloat16):
    level = block_levels(stream_key, shape, cuts, -0.22, 0.18) if cuts else 1.0
    result = jax.random.normal(stream_key, shape, jnp.float32) * spread * level
    return jnp.minimum(jnp.maximum(result, -bound), bound).astype(held_as)


def setup_inputs(seed: int = 0) -> dict:
    key_list = jax.random.split(jax.random.key(seed), 11)
    inputs = scatter_about(key_list[0], (MB, ROWS_ALL, L, D), 1.0, 6.0, ((1, 16),))
    cotangent = scatter_about(key_list[1], (MB, ROWS_ALL, L, D), 1.0, 6.0, ((1, 16),))
    image_ids = jax.vmap(lambda own: jnp.searchsorted(jnp.cumsum(uneven_parts(own, 4, L, 3 * L // 8, 0)), jnp.arange(L), side="right"))(jax.random.split(key_list[2], MB * ROWS_ALL)).reshape((MB, ROWS_ALL, L)).astype(jnp.int32)
    keep_mask = draw_keep_mask(jax.random.fold_in(key_list[10], 71), 0)
    w_qkv = scatter_about(key_list[4], (2, 3, D, D), D ** -0.5, 0.21875, ((0, 2), (3, 4)))
    w_out = scatter_about(key_list[5], (2, D, D), (D // 16) ** -0.5, 0.875, ((0, 2), (1, 4)))
    w_up = scatter_about(key_list[6], (2, D, FF), D ** -0.5, 0.21875, ((0, 2), (2, 4)))
    w_down = scatter_about(key_list[7], (2, FF, D), FF ** -0.5, 0.109375, ((0, 2), (1, 4)))
    norm_gain = jnp.clip(1.0 + 0.1 * jax.random.normal(key_list[8], (2, 2, D), jnp.float32), 0.5, 1.5)
    norm_shift = scatter_about(key_list[9], (2, 2, D), 0.2, 1.0, ((0, 2),), jnp.float32)
    return dict(inputs=inputs, cotangent=cotangent, image_ids=image_ids, keep_mask=keep_mask, w_qkv=w_qkv, w_out=w_out, w_up=w_up, w_down=w_down, norm_gain=norm_gain, norm_shift=norm_shift)


@jax.custom_vjp
def low(v):
    return lax.optimization_barrier(v.astype(jnp.bfloat16)).astype(jnp.float32)

@jax.custom_vjp
def low_back(v):
    return v

def low_keep(v):
    return (low(v), None)

def low_pass(kept, grad):
    return (grad,)

def back_keep(v):
    return (v, None)

def back_low(kept, grad):
    return (low(grad),)
low.defvjp(low_keep, low_pass)
low_back.defvjp(back_keep, back_low)
highest = lax.Precision.HIGHEST
norm_eps = 1e-05
masked_score = -1e+30

def normalize(resid, gain, shift):
    mean_value = lax.optimization_barrier(jnp.mean(resid, axis=-1, keepdims=True))
    centered = resid - mean_value
    inv_std = lax.rsqrt(lax.optimization_barrier(jnp.mean(centered * centered, axis=-1, keepdims=True)) + norm_eps)
    return centered * inv_std * gain + shift

def layer(resid, select, allowed, w_qkv, w_out, w_up, w_down, gains, shifts):
    group_rows, length, features = resid.shape
    normed_one = low(normalize(resid, gains[0], shifts[0]))
    projected = low_back(low(jnp.einsum('gld,jde->jgle', normed_one, w_qkv, precision=highest)))
    head_parts = projected.reshape(3, group_rows, length, HEADS, HEAD)
    scores = low_back(jnp.einsum('gqhe,gkhe->ghqk', head_parts[0], head_parts[1], precision=highest) * HEAD ** (-0.5))
    scores = jnp.where(allowed[:, None], scores, masked_score)
    attention = low(jax.nn.softmax(scores, axis=-1))
    mixed_heads = low_back(low(jnp.einsum('ghqk,gkhe->gqhe', attention, head_parts[2], precision=highest)))
    attn_out = low_back(jnp.einsum('gle,ed->gld', mixed_heads.reshape(group_rows, length, features), w_out, precision=highest))
    middle = resid + select[..., None] * attn_out
    normed_two = low(normalize(middle, gains[1], shifts[1]))
    pre_act = low_back(jnp.einsum('gld,df->glf', normed_two, w_up, precision=highest))
    hidden = low(jax.nn.gelu(pre_act))
    mlp_out = low_back(jnp.einsum('glf,fd->gld', hidden, w_down, precision=highest))
    return middle + select[..., None] * mlp_out

def two_layers(params, block_in, block_probe, block_ids, block_keep):
    same_image = block_ids[:, :, None] == block_ids[:, None, :]
    diagonal = jnp.eye(block_ids.shape[1], dtype=bool)
    select = block_keep.astype(block_in.dtype)
    allowed = same_image & ((block_keep[:, None, :] > 0) | diagonal[None])
    first_out = layer(block_in, select, allowed, *[weight[0] for weight in params])
    second_in = low_back(low(first_out)) + block_probe
    second_out = layer(second_in, jnp.ones_like(select), same_image, *[weight[1] for weight in params])
    return (second_out, first_out)

def reference(inputs, cotangent, image_ids, keep_mask, w_qkv, w_out, w_up, w_down, norm_gain, norm_shift):
    total_rows = MB * ROWS_ALL
    group_size = math.gcd(total_rows, 16)
    blocks = total_rows // group_size

    def to_blocks(array):
        return array.reshape((blocks, group_size) + array.shape[2:])
    input_blocks = to_blocks(inputs.astype(jnp.float32))
    cot_blocks = to_blocks(cotangent.astype(jnp.float32))
    id_blocks = to_blocks(image_ids)
    keep_blocks = to_blocks(keep_mask)
    params = tuple((weight.astype(jnp.float32) for weight in (w_qkv, w_out, w_up, w_down, norm_gain, norm_shift)))
    probe_blocks = jnp.zeros_like(input_blocks)

    def forward(params, input_blocks, probe_blocks):

        def step(carry, block_items):
            second_out, first_out = jax.checkpoint(two_layers)(params, block_items[0], block_items[1], block_items[2], block_items[3])
            return (carry, (second_out, first_out))
        carry_zero = jnp.zeros((), input_blocks.dtype)
        _, outs_pair = lax.scan(step, carry_zero, (input_blocks, probe_blocks, id_blocks, keep_blocks))
        return (outs_pair[0], outs_pair[1])
    second_out, pullback, first_out = jax.vjp(forward, params, input_blocks, probe_blocks, has_aux=True)
    grad_params, grad_inputs, grad_probe = pullback(cot_blocks)
    shape_out = (MB, ROWS_ALL, L, D)
    layer_out = jnp.stack([first_out.reshape(shape_out), second_out.reshape(shape_out)]).astype(jnp.bfloat16)
    input_grad = jnp.stack([grad_inputs.reshape(shape_out), grad_probe.reshape(shape_out)])
    counts = lax.optimization_barrier(jnp.sum(keep_mask, axis=(0, 1))).astype(jnp.int32)
    return (layer_out, input_grad, grad_params[0], grad_params[1], grad_params[2], grad_params[3], grad_params[4], grad_params[5], counts)
```

```python
import functools

import jax
import jax.numpy as jnp
from jax import lax
from jax.experimental import pallas as pl
from jax.experimental.pallas import tpu as pltpu
from jax.sharding import PartitionSpec as P

HEAD = 64
KEEP = 52
EPS = 1e-05
MASKED = -1e30
BF = jnp.bfloat16
F32 = jnp.float32
MESH = pl.DeviceIdType.MESH
GELU_C = 0.7978845608028654
GELU_A = 0.044715
CHUNKS = 16
SKEW = 2


def dg(a, b, ca, cb):
    return lax.dot_general(a, b, (((ca,), (cb,)), ((), ())), preferred_element_type=F32)


def rows_at(start, size):
    return pl.ds(pl.multiple_of(start, 16), size)


def standardize(v):
    centered = v - jnp.mean(v, axis=-1, keepdims=True)
    inv = lax.rsqrt(jnp.mean(centered * centered, axis=-1, keepdims=True) + EPS)
    return centered * inv, inv


def norm_back(g, gain, xhat, inv):
    gg = g * gain
    inner = gg - jnp.mean(gg, axis=-1, keepdims=True)
    return inv * (inner - xhat * jnp.mean(gg * xhat, axis=-1, keepdims=True))


def gelu_pair(x):
    square = x * x
    th = jnp.tanh(GELU_C * (x + GELU_A * x * square))
    half = 0.5 * (1.0 + th)
    slope = half + (0.5 * GELU_C) * x * (1.0 - th * th) * (1.0 + 3.0 * GELU_A * square)
    return x * half, slope


def attend(qkv, row0, heads, n, mask, pt, p0, mix, m0):
    e = heads * HEAD
    for h in range(heads):
        q = qkv[rows_at(row0 + h * HEAD, HEAD), 0:n]
        k = qkv[rows_at(row0 + e + h * HEAD, HEAD), 0:n]
        v = qkv[rows_at(row0 + 2 * e + h * HEAD, HEAD), 0:n]
        s = jnp.where(mask, dg(k, q, 0, 0), MASKED)
        w = jnp.exp(s - jnp.max(s, axis=0, keepdims=True))
        p = (w * (1.0 / jnp.sum(w, axis=0, keepdims=True))).astype(BF)
        pt[rows_at(p0 + h * n, n), 0:n] = p
        mix[rows_at(m0 + h * HEAD, HEAD), 0:n] = dg(v, p, 1, 0).astype(BF)


def attend_back(qkv, row0, heads, n, pt, p0, dmix, d0):
    e = heads * HEAD
    for h in range(heads):
        qs = rows_at(row0 + h * HEAD, HEAD)
        ks = rows_at(row0 + e + h * HEAD, HEAD)
        vs = rows_at(row0 + 2 * e + h * HEAD, HEAD)
        q, k, v = qkv[qs, 0:n], qkv[ks, 0:n], qkv[vs, 0:n]
        p = pt[rows_at(p0 + h * n, n), 0:n]
        dm = dmix[rows_at(d0 + h * HEAD, HEAD), 0:n]
        dp = dg(v, dm, 0, 0)
        pf = p.astype(F32)
        ds = (pf * (dp - jnp.sum(dp * pf, axis=0, keepdims=True))).astype(BF)
        qkv[vs, 0:n] = dg(dm, p, 1, 1).astype(BF)
        qkv[ks, 0:n] = dg(q, ds, 1, 1).astype(BF)
        qkv[qs, 0:n] = (dg(k, ds, 1, 0) * (HEAD ** -0.5)).astype(BF)


def body(
    n_dp,
    x_ref, cot_ref, ids_ref, keep_ref, wqkv_ref, wout_ref, wup_ref, wdown_ref, gain_ref, shift_ref,
    lo_ref, ig_ref, g_ref, st_ref,
    wt, wo2, rank, psel, n1, qkv, pt, mix, pa, ra, mid, u, n2, hid, gp, dm, pd, rcd, ryd, pm, rcm, rym,
    dat, dmx, rn, dmid, g, g2, r2, ra_ar, rb_ar, rx, gs, gf, stt, stz,
    ssem, rsem, sup, sdn, sra, srb, sts, str_, szs, szr, osem,
):
    s, z, t = lax.axis_index("section"), lax.axis_index("dp"), lax.axis_index("tensor")
    micro, length, feat = x_ref.shape
    n_t = 4
    c = lax.rem(t, 2)
    y = t // 2
    tc = t + 1 - 2 * c
    ty = lax.rem(t + 2, n_t)
    td = lax.rem(tc + 2, n_t)
    core_dev, y_dev, x_dev = (s, z, tc), (s, z, ty), (1 - s, z, t)
    e = wout_ref.shape[0]
    heads = e // HEAD
    ff = wup_ref.shape[1]
    n0 = -(-micro * KEEP // 16) * 16

    def remote(src, dst, ci, k, dev):
        return pltpu.make_async_remote_copy(
            src_ref=src, dst_ref=dst, send_sem=ssem.at[ci, k], recv_sem=rsem.at[ci, k],
            device_id=dev, device_id_type=MESH)

    bar = pltpu.get_barrier_semaphore()
    for dev in (core_dev, y_dev, (s, z, td), x_dev):
        pl.semaphore_signal(bar, inc=1, device_id=dev, device_id_type=MESH)

    @pl.loop(1, n_dp)
    def _(i):
        pl.semaphore_signal(bar, inc=1, device_id=(s, lax.rem(z + i, n_dp), t), device_id_type=MESH)

    below = lax.broadcasted_iota(jnp.int32, (length, length), 0)
    tri = jnp.where(below <= lax.broadcasted_iota(jnp.int32, (length, length), 1), 1.0, 0.0).astype(BF)
    keep8 = keep_ref[...].astype(F32)
    rank[...] = jnp.where(keep8 > 0.5, dg(keep8.astype(BF), tri, 1, 0), -1e6)
    spot = lax.broadcasted_iota(jnp.int32, (n0, length), 0).astype(F32) + 1.0

    def picker(row, m):
        return jnp.where(rank[pl.ds(row, 1), :] == spot - float(KEEP * m), 1.0, 0.0).astype(BF)

    for m in range(micro):
        psel[m] = picker(m * n_t + t, m)
    image = lax.broadcasted_iota(jnp.int32, (8, length), 0)

    def image_hot(row, shift):
        return jnp.where(ids_ref[pl.ds(row, 1), :] == image - shift, 1.0, 0.0).astype(BF)

    def same(hot):
        return dg(hot, hot, 0, 0) > 0.5

    def kept_column(m):
        return dg(psel[m], jnp.ones((n0, 128), BF), 0, 0)[:, 0:1] > 0.5

    def transpose_weights():
        for j in range(3):
            wt[j * e:(j + 1) * e, :] = wqkv_ref[j].T

    gain = [gain_ref[j:j + 1, :] for j in range(2)]
    shift = [shift_ref[j:j + 1, :] for j in range(2)]
    pl.semaphore_wait(bar, 4 + n_dp - 1)

    sends = []

    def go(copy):
        copy.start()
        sends.append(copy)

    def gather_start(buf, blk, n, ci):
        own = buf.at[rows_at(blk(t) * n, n)]
        go(remote(own, own, ci, 1, y_dev))
        go(remote(own, own, ci, 0, core_dev))

    def arrived(buf, blk, n, ci, k):
        part = buf.at[rows_at(blk * n, n)]
        remote(part, part, ci, k, core_dev).wait_recv()

    def gather_core(buf, blk, n, ci):
        arrived(buf, blk(tc), n, ci, 0)

    def gather_pass(buf, blk, n, ci):
        arrived(buf, blk(ty), n, ci, 1)
        part = buf.at[rows_at(blk(ty) * n, n)]
        go(remote(part, part, ci, 2, core_dev))

    def gather_end(buf, blk, n, ci):
        arrived(buf, blk(td), n, ci, 2)

    def scatter_near(part, blk, n, ci, rc, r0):
        go(remote(part.at[rows_at(blk(tc) * n, n)], rc.at[rows_at(r0 + n, n)], ci, 1, core_dev))

    def scatter_far(part, blk, n, ci, rc, r0):
        go(remote(part.at[rows_at(blk(td) * n, n)], rc.at[rows_at(r0, n)], ci, 0, core_dev))

    def scatter_pass(part, blk, n, ci, rc, r0, ry, y0):
        first = rc.at[rows_at(r0, n)]
        remote(first, first, ci, 0, core_dev).wait_recv()
        mine = rows_at(blk(ty) * n, n)
        part[mine, :] = (part[mine, :].astype(F32) + rc[rows_at(r0, n), :].astype(F32)).astype(BF)
        go(remote(part.at[mine], ry.at[rows_at(y0, n)], ci, 2, y_dev))

    def scatter_end(part, blk, n, ci, rc, r0, ry, y0):
        second, last = rc.at[rows_at(r0 + n, n)], ry.at[rows_at(y0, n)]
        remote(second, second, ci, 1, core_dev).wait_recv()
        remote(last, last, ci, 2, y_dev).wait_recv()
        return (part[rows_at(blk(t) * n, n), :].astype(F32) + rc[rows_at(r0 + n, n), :].astype(F32)
                + ry[rows_at(y0, n), :].astype(F32))

    def mlp_rows(r, n):
        pre = dg(n2[rows_at(r, n), :], wup_ref[...], 1, 0)
        act, slope = gelu_pair(pre)
        hid[rows_at(r, n), :] = act.astype(BF)
        gp[rows_at(r, n), :] = slope.astype(BF)

    def mlp_back_rows(r, n, part):
        dh = dg(dm[rows_at(r, n), :], wdown_ref[...], 1, 1)
        dpre = (gp[rows_at(r, n), :].astype(F32) * dh).astype(BF)
        gp[rows_at(r, n), :] = dpre
        part[rows_at(r, n), :] = dg(dpre, wup_ref[...], 1, 1).astype(BF)

    def count_row(m):
        return keep_ref[pl.ds(m * n_t + t, 1), :].astype(F32)

    st_ref[...] = jnp.zeros(st_ref.shape, F32)
    st_ref[4:5, 0:length] = sum(count_row(m) for m in range(micro))

    @pl.when(s == 0)
    def _():
        n = n0
        ident = lambda b: b
        near, far = 2 * y, 2 - 2 * y
        xs = sum(dg(psel[m], x_ref[m], 1, 0) for m in range(micro))
        u[0:n, :] = xs.astype(BF)
        n1[rows_at(t * n, n), :] = (standardize(xs)[0] * gain[0] + shift[0]).astype(BF)
        gather_start(n1, ident, n, 0)
        transpose_weights()

        def block_hot(b):
            return sum(dg(image_hot(m * n_t + b, 4 * m), picker(m * n_t + b, m), 1, 1)
                       for m in range(micro)).astype(BF)

        def forward(b):
            r = b * 3 * e
            proj = dg(wt[0:3 * e, :], n1[rows_at(b * n, n), :], 1, 1)
            qkv[rows_at(r, e), 0:n] = (proj[0:e] * (HEAD ** -0.5)).astype(BF)
            qkv[rows_at(r + e, 2 * e), 0:n] = proj[e:].astype(BF)
            attend(qkv, r, heads, n, same(block_hot(b)), pt, b * heads * n, mix, b * e)
            pa[rows_at(b * n, n), :] = dg(mix[rows_at(b * e, e), 0:n], wout_ref[...], 0, 0).astype(BF)

        forward(t)
        gather_core(n1, ident, n, 0)
        forward(tc)
        scatter_near(pa, ident, n, 1, ra, 0)
        gather_pass(n1, ident, n, 0)
        forward(ty)
        gather_end(n1, ident, n, 0)
        forward(td)
        scatter_far(pa, ident, n, 1, ra, 0)
        scatter_pass(pa, ident, n, 1, ra, 0, rn, 0)
        middle = xs + scatter_end(pa, ident, n, 1, ra, 0, rn, 0)
        mid[0:n, :] = middle
        n2[rows_at(t * n, n), :] = (standardize(middle)[0] * gain[1] + shift[1]).astype(BF)
        gather_start(n2, ident, n, 2)

        def mlp_forward(r):
            mlp_rows(r, 2 * n)
            pm[rows_at(r, 2 * n), :] = dg(hid[rows_at(r, 2 * n), :], wdown_ref[...], 1, 0).astype(BF)

        gather_core(n2, ident, n, 2)
        mlp_forward(near * n)
        scatter_near(pm, ident, n, 3, rcm, 0)
        gather_pass(n2, ident, n, 2)
        gather_end(n2, ident, n, 2)
        mlp_forward(far * n)
        scatter_far(pm, ident, n, 3, rcm, 0)
        scatter_pass(pm, ident, n, 3, rcm, 0, rym, 0)
        result = (middle + scatter_end(pm, ident, n, 3, rcm, 0, rym, 0)).astype(BF)
        gs[0:n, :] = result
        go(remote(gs.at[0:n], rx.at[0:n], 4, 0, x_dev))
        for m in range(micro):
            lo_ref[m] = jnp.where(kept_column(m), dg(psel[m], result, 0, 0), x_ref[m].astype(F32)).astype(BF)

        for copy in sends:
            copy.wait_send()
        sends.clear()

        remote(rx.at[0:n], rx.at[0:n], 4, 1, x_dev).wait_recv()
        dm[rows_at(t * n, n), :] = rx[0:n, :]
        gather_start(dm, ident, n, 5)
        gather_core(dm, ident, n, 5)
        mlp_back_rows(near * n, 2 * n, pd)
        scatter_near(pd, ident, n, 6, rcd, 0)
        gather_pass(dm, ident, n, 5)
        gather_end(dm, ident, n, 5)
        mlp_back_rows(far * n, 2 * n, pd)
        scatter_far(pd, ident, n, 6, rcd, 0)
        scatter_pass(pd, ident, n, 6, rcd, 0, ryd, 0)
        every = slice(0, n_t * n)
        g[0:ff, :] = dg(hid[every, :], dm[every, :], 0, 0).astype(BF)
        g[rows_at(ff, feat), :] = dg(n2[every, :], gp[every, :], 0, 0).astype(BF)
        d_two = scatter_end(pd, ident, n, 6, rcd, 0, ryd, 0)
        xhat, inv = standardize(mid[0:n, :])
        st_ref[1:2, :] = jnp.sum(d_two * xhat, axis=0, keepdims=True)
        st_ref[3:4, :] = jnp.sum(d_two, axis=0, keepdims=True)
        d_mid = rx[0:n, :].astype(F32) + norm_back(d_two, gain[1], xhat, inv)
        dat[rows_at(t * n, n), :] = d_mid.astype(BF)
        gather_start(dat, ident, n, 7)

        def backward(b):
            r = b * 3 * e
            dmx[0:e, 0:n] = dg(wout_ref[...], dat[rows_at(b * n, n), :], 1, 1).astype(BF)
            attend_back(qkv, r, heads, n, pt, b * heads * n, dmx, 0)
            pa[rows_at(b * n, n), :] = dg(qkv[rows_at(r, 3 * e), 0:n], wt[0:3 * e, :], 0, 0).astype(BF)

        backward(t)
        gather_core(dat, ident, n, 7)
        backward(tc)
        scatter_near(pa, ident, n, 8, rcm, 2 * n)
        gather_pass(dat, ident, n, 7)
        backward(ty)
        gather_end(dat, ident, n, 7)
        backward(td)
        scatter_far(pa, ident, n, 8, rcm, 2 * n)
        scatter_pass(pa, ident, n, 8, rcm, 2 * n, rym, n)
        g[rows_at(ff + feat, e), :] = sum(
            dg(mix[b * e:(b + 1) * e, 0:n], dat[b * n:(b + 1) * n, :], 1, 0) for b in range(n_t)).astype(BF)
        g[rows_at(ff + feat + e, 3 * e), :] = sum(
            dg(qkv[b * 3 * e:(b + 1) * 3 * e, 0:n], n1[b * n:(b + 1) * n, :], 1, 0) for b in range(n_t)).astype(BF)
        d_one = scatter_end(pa, ident, n, 8, rcm, 2 * n, rym, n)
        xhat, inv = standardize(u[0:n, :].astype(F32))
        st_ref[0:1, :] = jnp.sum(d_one * xhat, axis=0, keepdims=True)
        st_ref[2:3, :] = jnp.sum(d_one, axis=0, keepdims=True)
        got = d_mid + norm_back(d_one, gain[0], xhat, inv)
        high = got.astype(BF)
        low = (got - high.astype(F32)).astype(BF)
        for m in range(micro):
            whole = gf.at[rows_at(m * length, length)]
            remote(whole, whole, 9, m, x_dev).wait_recv()
            ig_ref[m] = jnp.where(kept_column(m), dg(psel[m], high, 0, 0) + dg(psel[m], low, 0, 0),
                                  gf[rows_at(m * length, length), :].astype(F32))
        for copy in sends:
            copy.wait_send()
        sends.clear()

    @pl.when(s == 1)
    def _():
        n = length
        transpose_weights()
        go(remote(wt.at[0:3 * e], wt.at[3 * e:6 * e], 0, 0, y_dev))
        go(remote(wout_ref, wo2, 0, 1, y_dev))
        at = [lambda b, m=m: m * n_t + b for m in range(micro)]
        for m in range(micro):
            dm[rows_at(at[m](t) * n, n), :] = cot_ref[m]
            gather_start(dm, at[m], n, 1 + m)
        for m in range(micro):
            gather_core(dm, at[m], n, 1 + m)
        for m in range(micro):
            gather_pass(dm, at[m], n, 1 + m)
        for m in range(micro):
            gather_end(dm, at[m], n, 1 + m)
        remote(wt.at[3 * e:6 * e], wt.at[3 * e:6 * e], 0, 0, y_dev).wait_recv()
        remote(wo2, wo2, 0, 1, y_dev).wait_recv()

        def mine(m):
            return 2 * m + c

        def peer(m):
            return 2 * m + 1 - c

        remote(rx.at[0:n0], rx.at[0:n0], 4, 0, x_dev).wait_recv()
        for m in range(micro):
            u1 = jnp.where(kept_column(m), dg(psel[m], rx[0:n0, :], 0, 0), x_ref[m].astype(F32))
            u[rows_at(m * n, n), :] = u1.astype(BF)
            n1[rows_at(mine(m) * n, n), :] = (standardize(u1)[0] * gain[0] + shift[0]).astype(BF)
            block = n1.at[rows_at(mine(m) * n, n)]
            go(remote(block, block, 3, m, core_dev))

        def forward(b, m, owner):
            r = b * 6 * e
            mask = same(image_hot(m * n_t + owner, 0))
            proj = dg(wt[...], n1[rows_at(b * n, n), :], 1, 1)
            for j in range(2):
                a = j * 3 * e
                qkv[rows_at(r + a, e), 0:n] = (proj[a:a + e] * (HEAD ** -0.5)).astype(BF)
                qkv[rows_at(r + a + e, 2 * e), 0:n] = proj[a + e:a + 3 * e].astype(BF)
            for j in range(2):
                attend(qkv, r + j * 3 * e, heads, n, mask, pt, (b * 2 + j) * heads * n, mix, (b * 2 + j) * e)
            pa[rows_at(b * n, n), :] = (
                dg(mix[rows_at(b * 2 * e, e), 0:n], wout_ref[...], 0, 0)
                + dg(mix[rows_at(b * 2 * e + e, e), 0:n], wo2[...], 0, 0)).astype(BF)

        for m in range(micro):
            block = n1.at[rows_at(peer(m) * n, n)]
            remote(block, block, 3, m, core_dev).wait_recv()
            forward(peer(m), m, tc)
            go(remote(pa.at[rows_at(peer(m) * n, n)], ra.at[rows_at(m * n, n)], 5, m, core_dev))
            forward(mine(m), m, t)
            got = ra.at[rows_at(m * n, n)]
            remote(got, got, 5, m, core_dev).wait_recv()
            middle = (u[rows_at(m * n, n), :].astype(F32) + pa[rows_at(mine(m) * n, n), :].astype(F32)
                      + ra[rows_at(m * n, n), :].astype(F32))
            mid[rows_at(m * n, n), :] = middle
            n2[rows_at(at[m](t) * n, n), :] = (standardize(middle)[0] * gain[1] + shift[1]).astype(BF)
            gather_start(n2, at[m], n, 6 + m)

        near, far = 2 * y, 2 - 2 * y
        for m in range(micro):
            gather_core(n2, at[m], n, 6 + m)
            r = at[m](near) * n
            mlp_rows(r, 2 * n)
            mlp_back_rows(r, 2 * n, pd)
            scatter_near(pd, at[m], n, 8 + m, rcd, m * 2 * n)
            gather_pass(n2, at[m], n, 6 + m)
        for m in range(micro):
            gather_end(n2, at[m], n, 6 + m)
            r = at[m](far) * n
            mlp_rows(r, 2 * n)
            mlp_back_rows(r, 2 * n, pd)
            scatter_far(pd, at[m], n, 8 + m, rcd, m * 2 * n)
            scatter_pass(pd, at[m], n, 8 + m, rcd, m * 2 * n, ryd, m * n)

        @pl.loop(0, micro)
        def _(m):
            r = m * n_t * n
            pm[rows_at(r, n_t * n), :] = dg(hid[rows_at(r, n_t * n), :], wdown_ref[...], 1, 0).astype(BF)

        for m in range(micro):
            scatter_near(pm, at[m], n, 10 + m, rcm, m * 2 * n)
            scatter_far(pm, at[m], n, 10 + m, rcm, m * 2 * n)
        every = slice(0, micro * n_t * n)
        g[0:ff, :] = dg(hid[every, :], dm[every, :], 0, 0).astype(BF)
        for m in range(micro):
            scatter_pass(pm, at[m], n, 10 + m, rcm, m * 2 * n, rym, m * n)
        g[rows_at(ff, feat), :] = dg(n2[every, :], gp[every, :], 0, 0).astype(BF)

        stats = [jnp.zeros((1, feat), F32) for _ in range(4)]
        for m in range(micro):
            d_two = scatter_end(pd, at[m], n, 8 + m, rcd, m * 2 * n, ryd, m * n)
            xhat, inv = standardize(mid[rows_at(m * n, n), :])
            stats[1] += jnp.sum(d_two * xhat, axis=0, keepdims=True)
            stats[3] += jnp.sum(d_two, axis=0, keepdims=True)
            d_mid = cot_ref[m].astype(F32) + norm_back(d_two, gain[1], xhat, inv)
            dmid[rows_at(m * n, n), :] = d_mid
            dat[rows_at(mine(m) * n, n), :] = d_mid.astype(BF)
            block = dat.at[rows_at(mine(m) * n, n)]
            go(remote(block, block, 12, m, core_dev))

        def backward(b):
            r = b * 6 * e
            d_rows = dat[rows_at(b * n, n), :]
            dmx[0:e, 0:n] = dg(wout_ref[...], d_rows, 1, 1).astype(BF)
            dmx[e:2 * e, 0:n] = dg(wo2[...], d_rows, 1, 1).astype(BF)
            for j in range(2):
                attend_back(qkv, r + j * 3 * e, heads, n, pt, (b * 2 + j) * heads * n, dmx, j * e)
            pd[rows_at(b * n, n), :] = dg(qkv[rows_at(r, 6 * e), 0:n], wt[...], 0, 0).astype(BF)

        for copy in sends:
            copy.wait_send()
        sends.clear()
        for m in range(micro):
            block = dat.at[rows_at(peer(m) * n, n)]
            remote(block, block, 12, m, core_dev).wait_recv()
            backward(peer(m))
            go(remote(pd.at[rows_at(peer(m) * n, n)], rn.at[rows_at(m * n, n)], 13, m, core_dev))
            backward(mine(m))
            got = rn.at[rows_at(m * n, n)]
            remote(got, got, 13, m, core_dev).wait_recv()
            d_one = pd[rows_at(mine(m) * n, n), :].astype(F32) + rn[rows_at(m * n, n), :].astype(F32)
            xhat, inv = standardize(u[rows_at(m * n, n), :].astype(F32))
            stats[0] += jnp.sum(d_one * xhat, axis=0, keepdims=True)
            stats[2] += jnp.sum(d_one, axis=0, keepdims=True)
            in_grad = dmid[rows_at(m * n, n), :] + norm_back(d_one, gain[0], xhat, inv)
            ig_ref[m] = in_grad
            gf[rows_at(m * n, n), :] = in_grad.astype(BF)
        gs[0:n0, :] = sum(dg(psel[m], gf[rows_at(m * n, n), :], 1, 0) for m in range(micro)).astype(BF)
        go(remote(gs.at[0:n0], rx.at[0:n0], 4, 1, x_dev))
        for m in range(micro):
            whole = gf.at[rows_at(m * n, n)]
            go(remote(whole, whole, 9, m, x_dev))
        for j in range(4):
            st_ref[j:j + 1, :] = stats[j]

        blocks = 2 * micro

        def qkv_grad(j):
            return sum(dg(qkv[b * 6 * e + j * 3 * e:b * 6 * e + (j + 1) * 3 * e, 0:n],
                          n1[b * n:(b + 1) * n, :], 1, 0) for b in range(blocks))

        def out_grad(j):
            return sum(dg(mix[(2 * b + j) * e:(2 * b + j + 1) * e, 0:n],
                          dat[b * n:(b + 1) * n, :], 1, 0) for b in range(blocks))

        g2[0:e, :] = out_grad(1).astype(BF)
        g2[e:4 * e, :] = qkv_grad(1).astype(BF)
        go(remote(g2, r2, 14, 0, y_dev))
        own_out = out_grad(0)
        own_qkv = qkv_grad(0)
        remote(r2, r2, 14, 0, y_dev).wait_recv()
        g[rows_at(ff + feat, e), :] = (own_out + r2[0:e, :].astype(F32)).astype(BF)
        g[rows_at(ff + feat + e, 3 * e), :] = (own_qkv + r2[e:4 * e, :].astype(F32)).astype(BF)
        for m in range(micro):
            mlp = scatter_end(pm, at[m], n, 10 + m, rcm, m * 2 * n, rym, m * n)
            lo_ref[m] = (mid[rows_at(m * n, n), :] + mlp).astype(BF)
        for copy in sends:
            copy.wait_send()
        sends.clear()

    def exchange(buf, own, count, dev, send, recv):
        @pl.loop(1, count)
        def _(i):
            pltpu.make_async_remote_copy(
                src_ref=buf.at[own], dst_ref=buf.at[own], send_sem=send.at[i], recv_sem=recv.at[i],
                device_id=dev(lax.rem(own + i, count)), device_id_type=MESH).start()

        @pl.loop(1, count)
        def _(i):
            other = lax.rem(own + count - i, count)
            pltpu.make_async_remote_copy(
                src_ref=buf.at[other], dst_ref=buf.at[other], send_sem=send.at[i], recv_sem=recv.at[i],
                device_id=dev(other), device_id_type=MESH).wait()

    stt[t] = st_ref[...]
    exchange(stt, t, n_t, lambda i: (s, z, i), sts, str_)
    stz[z] = sum(stt[i] for i in range(n_t))
    exchange(stz, z, n_dp, lambda i: (s, i, t), szs, szr)
    st_ref[...] = sum(stz[i] for i in range(n_dp))

    size = g.shape[0] // CHUNKS
    half = n_dp // 2
    inward = jnp.where(z < half, 1, -1)
    inner, outer = lax.rem(z + inward + n_dp, n_dp), lax.rem(z - inward + n_dp, n_dp)
    is_edge = (z == 0) | (z == n_dp - 1)
    is_mid = (z == half - 1) | (z == half)

    def chunk(i):
        return rows_at(i * size, size)

    def to_inner(i, dst, sem):
        return pltpu.make_async_remote_copy(
            src_ref=g.at[chunk(i)], dst_ref=dst.at[chunk(i)], send_sem=sup.at[i], recv_sem=sem.at[i],
            device_id=(s, inner, t), device_id_type=MESH)

    def to_outer(i):
        return pltpu.make_async_remote_copy(
            src_ref=rb_ar.at[chunk(i)], dst_ref=rb_ar.at[chunk(i)], send_sem=sdn.at[i], recv_sem=srb.at[i],
            device_id=(s, outer, t), device_id_type=MESH)

    @pl.loop(0, CHUNKS + SKEW)
    def _(i):
        @pl.when(i < CHUNKS)
        def _():
            @pl.when(jnp.logical_not(is_edge))
            def _():
                to_inner(i, ra_ar, sra).wait_recv()
                g[chunk(i), :] = (g[chunk(i), :].astype(F32) + ra_ar[chunk(i), :].astype(F32)).astype(BF)

            @pl.when(is_mid)
            def _():
                to_inner(i, rb_ar, srb).start()

            @pl.when(jnp.logical_not(is_mid))
            def _():
                to_inner(i, ra_ar, sra).start()

        @pl.when(i >= SKEW)
        def _():
            k = i - SKEW
            to_outer(k).wait_recv()

            @pl.when(is_mid)
            def _():
                rb_ar[chunk(k), :] = (g[chunk(k), :].astype(F32) + rb_ar[chunk(k), :].astype(F32)).astype(BF)

            @pl.when(jnp.logical_not(is_edge))
            def _():
                to_outer(k).start()

    @pl.loop(0, CHUNKS)
    def _(i):
        to_inner(i, ra_ar, sra).wait_send()

        @pl.when(jnp.logical_not(is_edge))
        def _():
            to_outer(i).wait_send()

    out = pltpu.make_async_copy(rb_ar, g_ref, osem)
    out.start()
    out.wait()


def on_device(
    inputs, cotangent, image_ids, keep_mask, w_qkv, w_out, w_up, w_down, norm_gain, norm_shift
):
    micro, share, length, feat = inputs.shape
    n_dp = lax.axis_size("dp")
    n_t = lax.axis_size("tensor")
    e = w_out.shape[1]
    ff = w_up.shape[2]
    n0 = -(-micro * KEEP // 16) * 16
    own, chip, full = micro * length, 2 * micro * length, n_t * micro * length
    heads = e // HEAD
    g_rows = ff + feat + 4 * e
    vmem = pltpu.VMEM
    dma = pltpu.SemaphoreType.DMA
    scratch = [
        vmem((6 * e, feat), BF),
        vmem((e, feat), BF),
        vmem((micro * n_t, length), F32),
        vmem((micro, n0, length), BF),
        vmem((chip, feat), BF),
        vmem((2 * micro * 6 * e, length), BF),
        vmem((2 * micro * 2 * heads * length, length), BF),
        vmem((2 * micro * 2 * e, length), BF),
        vmem((chip, feat), BF),
        vmem((own, feat), BF),
        vmem((own, feat), F32),
        vmem((own, feat), BF),
        vmem((full, feat), BF),
        vmem((full, ff), BF),
        vmem((full, ff), BF),
        vmem((full, feat), BF),
        vmem((full, feat), BF),
        vmem((2 * own, feat), BF),
        vmem((own, feat), BF),
        vmem((full, feat), BF),
        vmem((2 * own, feat), BF),
        vmem((own, feat), BF),
        vmem((chip, feat), BF),
        vmem((2 * e, length), BF),
        vmem((own, feat), BF),
        vmem((own, feat), F32),
        vmem((g_rows, feat), BF),
        vmem((4 * e, feat), BF),
        vmem((4 * e, feat), BF),
        vmem((g_rows, feat), BF),
        vmem((g_rows, feat), BF),
        vmem((n0, feat), BF),
        vmem((n0, feat), BF),
        vmem((own, feat), BF),
        vmem((n_t, 8, feat), F32),
        vmem((n_dp, 8, feat), F32),
        dma((15, 3)), dma((15, 3)),
        dma((CHUNKS,)), dma((CHUNKS,)), dma((CHUNKS,)), dma((CHUNKS,)),
        dma((n_t,)), dma((n_t,)), dma((n_dp,)), dma((n_dp,)),
        dma,
    ]
    in_vmem = pl.BlockSpec(memory_space=pltpu.VMEM)
    layer_out, input_grad, grads, stats = pl.pallas_call(
        functools.partial(body, n_dp),
        out_shape=(
            jax.ShapeDtypeStruct((micro, length, feat), BF),
            jax.ShapeDtypeStruct((micro, length, feat), F32),
            jax.ShapeDtypeStruct((g_rows, feat), BF),
            jax.ShapeDtypeStruct((8, feat), F32),
        ),
        in_specs=[in_vmem] * 10,
        out_specs=(in_vmem, in_vmem, pl.BlockSpec(memory_space=pl.ANY), in_vmem),
        scratch_shapes=scratch,
        compiler_params=pltpu.CompilerParams(
            collective_id=0, has_side_effects=True, vmem_limit_bytes=64 * 2 ** 20),
    )(
        inputs.reshape(micro, length, feat), cotangent.reshape(micro, length, feat),
        image_ids.reshape(-1, length), keep_mask.reshape(-1, length),
        w_qkv[0], w_out[0], w_up[0], w_down[0], norm_gain[0], norm_shift[0],
    )
    up, out, qkv = ff, ff + feat, ff + feat + e
    return (
        layer_out.reshape(1, micro, share, length, feat),
        input_grad.reshape(1, micro, share, length, feat),
        grads[qkv:].reshape(3, e, feat).transpose(0, 2, 1).astype(F32)[None],
        grads[out:qkv].astype(F32)[None],
        grads[up:out].astype(F32)[None],
        grads[:up].astype(F32)[None],
        stats[0:2][None],
        stats[2:4][None],
        stats[4, :length].astype(jnp.int32),
    )


def solution(mesh):
    in_specs = (
        P(None, ("dp", "tensor"), None, None),
        P(None, ("dp", "tensor"), None, None),
        P(None, "dp", None),
        P(None, "dp", None),
        P("section", None, None, "tensor"),
        P("section", "tensor", None),
        P("section", None, "tensor"),
        P("section", "tensor", None),
        P("section", None, None),
        P("section", None, None),
    )
    out_specs = (
        P("section", None, ("dp", "tensor"), None, None),
        P("section", None, ("dp", "tensor"), None, None),
        P("section", None, None, "tensor"),
        P("section", "tensor", None),
        P("section", None, "tensor"),
        P("section", "tensor", None),
        P("section", None, None),
        P("section", None, None),
        P(),
    )
    return jax.shard_map(
        on_device, mesh=mesh, in_specs=in_specs, out_specs=out_specs, check_vma=False
    )
```
